1024 devices in a mesh: blk: 64 (over z, core), sub: 16 (over x, y).
Axes of the slice: x: 4, y: 4, z: 32, core: 2. Of those that a mesh axis runs over, the one named last changes fastest.
Arguments:
- tracer: float32 [4, 28, 131072], P(None, None, ('blk', 'sub')), may hold values from 0 to 2
- edge_flow: float32 [28, 393216], P(None, ('blk', 'sub')), may hold values from -2.7 to 2.7
- edge_owner: int32 [393216], P(('blk', 'sub')), may hold values from 0 to 127
- edge_other: int32 [393216], P(('blk', 'sub')), may hold values from 0 to 255
- stencil: int32 [2, 16, 393216], P(None, None, ('blk', 'sub')), may hold values from 0 to 255
- stencil_coef: float32 [2, 16, 393216], P(None, None, ('blk', 'sub')), may hold values from -6 to 6
- stencil_count: int32 [2, 393216], P(None, ('blk', 'sub')), may hold values from 10 to 16
- send_cells: int32 [8, 16384], P(None, ('blk', 'sub')), may hold values from 0 to 127
- cell_area: float32 [131072], P(('blk', 'sub')), may hold values from 0.5 to 18, as said below
Outputs:
- advected: float32 [4, 28, 131072], P(None, None, ('blk', 'sub'))
- mass_mean: float32 [4, 28], replicated
The draws below stay inside these ranges and needn't reach their ends.
Inputs may be any that keep to these rules, and one draw needn't show every extreme that they name: `cell_area`: areas of the cells; positive.
All inputs are finite; a program needn't handle non-finite values.
Results may differ from the reference program's by a relative error of at most 0.00018.
Values sent between devices are 32-bit elements; how exact they have to be, the bound alone decides.
No kernel may reach another device: no remote copies, remote signals or barrier semaphores. Data moves between devices by JAX's collectives and lax.ppermute only.
A program may use at most 64 MiB of HBM per device.

```python
import jax
import jax.numpy as jnp
from jax import lax

NT = 4
NL = 28
STENCIL = 16
CELL_DEV = 128
PEER = 16
EDGE_DEV = 384
BLOCKS = 1024
NCELL = 131072
NEDGE = 393216
NSEND = 16384
N_SUB = 16


def draw_cell_area(key, part):
    key = jax.random.fold_in(key, 11)
    block_index = jnp.arange(NCELL) // CELL_DEV
    position = block_index.astype(jnp.float32) / max(BLOCKS - 1, 1)
    roughness = jax.random.uniform(key, (NCELL,), jnp.float32)
    widest = 3.0
    return widest ** position * 2.0 ** (2.0 * roughness - 1.0)


def place_ends(entries, stream_key, least, largest):
    longest = entries.shape.index(max(entries.shape))
    spots = []
    for shift in (0, 1):
        where = [jax.random.randint(jax.random.fold_in(stream_key, axis), (), 0, length) for axis, length in enumerate(entries.shape)]
        where[longest] = (where[longest] + shift) % entries.shape[longest]
        spots.append(tuple(where))
    return entries.at[spots[0]].set(least).at[spots[1]].set(largest)


def steps_of(rng, dims, cuts, smallest, high):
    gain, own = 1.0, jax.random.fold_in(rng, 6)
    for dim, shards_of in cuts:
        steps = jnp.exp(jax.random.uniform(jax.random.fold_in(own, dim), (shards_of,), jnp.float32, smallest / len(cuts), high / len(cuts)))
        gain = gain * jnp.repeat(steps, dims[dim] // shards_of).reshape([-1 if axis == dim else 1 for axis in range(len(dims))])
    return gain


def normal_values(stream_key, shape, width, reach, split=(), kind=jnp.bfloat16):
    entries = width * jax.random.normal(stream_key, shape, jnp.float32)
    if split:
        entries = entries * steps_of(stream_key, shape, split, -0.22, 0.18)
    return jnp.clip(entries, -reach, reach).astype(kind)


def setup_inputs(seed: int = 0) -> dict:
    streams_of = jax.random.split(jax.random.key(seed), 10)
    tracer = jnp.clip(2.0 * jax.random.uniform(streams_of[0], (NT, NL, NCELL), jnp.float32) ** steps_of(streams_of[0], (NT, NL, NCELL), ((2, 1024),), -0.2, 0.2), 0.0, 2.0)
    edge_flow = normal_values(streams_of[1], (NL, NEDGE), 0.9, 2.7, ((1, 1024),), jnp.float32)
    edge_owner = place_ends(jax.random.randint(streams_of[2], (NEDGE,), 0, CELL_DEV), jax.random.fold_in(streams_of[2], 1), 0, CELL_DEV - 1).astype(jnp.int32)
    edge_other = place_ends(jax.random.randint(streams_of[3], (NEDGE,), 0, CELL_DEV + 8 * PEER), jax.random.fold_in(streams_of[3], 1), 0, (CELL_DEV + 8 * PEER) - 1).astype(jnp.int32)
    stencil = place_ends(jax.random.randint(streams_of[4], (2, STENCIL, NEDGE), 0, CELL_DEV + 8 * PEER), jax.random.fold_in(streams_of[4], 1), 0, (CELL_DEV + 8 * PEER) - 1).astype(jnp.int32)
    stencil_coef = normal_values(streams_of[5], (2, STENCIL, NEDGE), 1.0, 6.0, ((2, 1024),), jnp.float32)
    stencil_count = place_ends(jax.random.randint(streams_of[6], (2, NEDGE), 10, STENCIL + 1), jax.random.fold_in(streams_of[6], 1), 10, STENCIL).astype(jnp.int32)
    send_cells = place_ends(jax.random.randint(streams_of[7], (8, NSEND), 0, CELL_DEV), jax.random.fold_in(streams_of[7], 1), 0, CELL_DEV - 1).astype(jnp.int32)
    cell_area = draw_cell_area(jax.random.fold_in(streams_of[9], 71), 0)
    return {"tracer": tracer, "edge_flow": edge_flow, "edge_owner": edge_owner, "edge_other": edge_other, "stencil": stencil, "stencil_coef": stencil_coef, "stencil_count": stencil_count, "send_cells": send_cells, "cell_area": cell_area}


def reference(tracer, edge_flow, edge_owner, edge_other, stencil, stencil_coef, stencil_count, send_cells, cell_area):
    columns = NT * NL
    extent = CELL_DEV + 8 * PEER
    offsets = jnp.array([-N_SUB - 1, -N_SUB, -N_SUB + 1, -1, 1, N_SUB - 1, N_SUB, N_SUB + 1], jnp.int32)
    opposite = (7 - jnp.arange(8)).astype(jnp.int32)
    live = jnp.arange(STENCIL, dtype=jnp.int32)[None, :, None] < stencil_count[:, None, :]
    weights = jnp.where(live, stencil_coef, jnp.zeros_like(stencil_coef))
    flow_dev = edge_flow.reshape(NL, BLOCKS, EDGE_DEV).transpose(1, 2, 0)
    owner_dev = edge_owner.reshape(BLOCKS, EDGE_DEV)
    other_dev = edge_other.reshape(BLOCKS, EDGE_DEV)
    sten_dev = stencil.reshape(2, STENCIL, BLOCKS, EDGE_DEV).transpose(2, 0, 1, 3)
    weight_dev = weights.reshape(2, STENCIL, BLOCKS, EDGE_DEV).transpose(2, 0, 1, 3)
    area_dev = cell_area.reshape(BLOCKS, CELL_DEV)
    send_dev = send_cells.reshape(8, BLOCKS, PEER).transpose(1, 0, 2)
    peers = (jnp.arange(BLOCKS, dtype=jnp.int32)[:, None] + offsets[None, :]) % BLOCKS
    source = (peers[:, :, None] * CELL_DEV + send_dev[peers, opposite[None, :]]).astype(jnp.int32)

    def one_block(items):
        own_rows, halo_rows, flow_b, owner_b, other_b, sten_b, weight_b, area_b = items
        extended = jnp.concatenate([own_rows, halo_rows], axis=0)
        first = extended[owner_b]
        second = extended[other_b]
        curves = []
        for side in range(2):
            gathered = extended[sten_b[side]]
            curves.append(jnp.sum(weight_b[side][:, :, None] * gathered, axis=0))
        flow_cols = jnp.tile(flow_b, (1, NT))
        flux = flow_cols * (first + second) / 2.0 - flow_cols * (curves[0] + curves[1]) / 12.0 + jnp.abs(flow_cols) * (curves[0] - curves[1]) / 12.0
        gained = jax.ops.segment_sum(flux, other_b, num_segments=extent)[:CELL_DEV]
        lost = jax.ops.segment_sum(flux, owner_b, num_segments=CELL_DEV)
        return (gained - lost) / area_b[:, None]

    def tendency(state):
        rows = state.reshape(columns, NCELL).T
        halo_rows = rows[source.reshape(-1)].reshape(BLOCKS, 8 * PEER, columns)
        own_rows = rows.reshape(BLOCKS, CELL_DEV, columns)
        change = lax.map(one_block, (own_rows, halo_rows, flow_dev, owner_dev, other_dev, sten_dev, weight_dev, area_dev))
        return change.reshape(NCELL, columns).T.reshape(NT, NL, NCELL)

    section_one = tracer + tendency(tracer) / 3.0
    section_two = tracer + tendency(section_one) / 2.0
    advected = tracer + tendency(section_two)
    weighted = jnp.sum(advected * cell_area[None, None, :], axis=2)
    mass_mean = weighted / jnp.sum(cell_area)
    return advected, mass_mean
```

```python
import functools

import jax
import jax.numpy as jnp
from jax import lax
from jax.experimental import pallas as pl
from jax.experimental.pallas import tpu as pltpu
from jax.sharding import PartitionSpec as P

F32 = jnp.float32
BF16 = jnp.bfloat16
PEER = 16
AXES = ("z", "core", "sub")


def split(x):
    hi = x.astype(BF16)
    return hi, (x - hi.astype(F32)).astype(BF16)


def dot(a, b):
    return lax.dot_general(a, b, (((1,), (0,)), ((), ())), preferred_element_type=F32)


def dot_nt(a, b):
    return lax.dot_general(a, b, (((1,), (1,)), ((), ())), preferred_element_type=F32)


def send_lanes(send_ref, wide_ref, backwards):
    groups, peer = send_ref.shape
    wide_ref[...] = jnp.zeros_like(wide_ref)
    wide_ref[:, :peer] = send_ref[...]
    lane = lax.broadcasted_iota(jnp.int32, (groups, 128), 1)
    group = lax.broadcasted_iota(jnp.int32, (groups, 128), 0)
    tiled = jnp.take_along_axis(wide_ref[...], lane % peer, axis=1)
    rows = []
    for back in backwards:
        want = groups - 1 - lane // peer if back else lane // peer
        rows.append(jnp.sum(jnp.where(want == group, tiled, 0), axis=0, keepdims=True))
    return rows


def square(rows):
    return jnp.concatenate([rows, jnp.zeros((128 - rows.shape[0], 128), F32)], axis=0)


def pick(state, lanes):
    return square(jnp.take_along_axis(state, jnp.broadcast_to(lanes, state.shape), axis=1)).T


def put_groups(out, next_ref, prev_ref, up_ref, down_ref):
    next_ref[:48] = jnp.concatenate([out[64:80], out[112:], out[32:48]], axis=0)
    prev_ref[:48] = jnp.concatenate([out[48:64], out[80:96], out[:16]], axis=0)
    up_ref[...] = out[96:112]
    down_ref[...] = out[16:32]


def put_rows(out, up_ref, down_ref, next_ref, prev_ref):
    up_ref[...] = out[80:]
    down_ref[...] = out[:48]
    next_ref[...] = out[64:80]
    prev_ref[...] = out[48:64]


def pack_kernel(tracer, send, stencil, coef, count, owner, other, flow, area,
                next_ref, prev_ref, up_ref, down_ref, lanes_ref, back_ref,
                tracer_ref, stencil_ref, coef_ref, count_ref, owner_ref, other_ref, flow_ref, area_ref,
                send_ref, wide_ref, owner_flat, other_flat, area_flat, sems):
    sources = (tracer, send, owner, other, area, stencil, coef, count, flow)
    targets = (tracer_ref, send_ref, owner_flat, other_flat, area_flat, stencil_ref, coef_ref, count_ref, flow_ref)
    copies = [pltpu.make_async_copy(a, b, sems.at[k]) for k, (a, b) in enumerate(zip(sources, targets))]
    for copy in copies:
        copy.start()
    copies[0].wait()
    copies[1].wait()
    lanes_ref[...], back_ref[...] = send_lanes(send_ref, wide_ref, (False, True))
    put_groups(pick(tracer_ref[...], lanes_ref[...]), next_ref, prev_ref, up_ref, down_ref)
    for copy in copies[2:]:
        copy.wait()
    owner_ref[...] = owner_flat[...].reshape(owner_ref.shape)
    other_ref[...] = other_flat[...].reshape(other_ref.shape)
    area_ref[...] = area_flat[...].reshape(area_ref.shape)


def fill(part, stencil_ref, coef_ref, count_ref, owner_ref, other_ref, mhi_ref, mlo_ref):
    edges = owner_ref.shape[1]
    for chunk in range(edges // 128):
        at = pl.ds(chunk * 128, 128)
        cell = lax.broadcasted_iota(jnp.int32, (128, 128), 0) + part * 128
        curves = []
        for side in range(2):
            total = jnp.zeros((128, 128), F32)
            count = count_ref[pl.ds(side, 1), at]
            for j in range(stencil_ref.shape[1]):
                weight = jnp.where(j < count, coef_ref[side, pl.ds(j, 1), at], 0.0)
                index = stencil_ref[side, pl.ds(j, 1), at]
                total = total + jnp.where(cell == index, weight, 0.0)
            curves.append(total)
        ends = jnp.where(cell == other_ref[:, at], 0.5, 0.0)
        if part == 0:
            ends = ends + jnp.where(cell == owner_ref[:, at], 0.5, 0.0)
        mean = ends - (curves[0] + curves[1]) * (1.0 / 12.0)
        diff = (curves[0] - curves[1]) * (1.0 / 12.0)
        for which, value in enumerate((mean, diff)):
            columns = pl.ds(which * edges + chunk * 128, 128)
            mhi_ref[:, columns], mlo_ref[:, columns] = split(value)


def own_kernel(stencil_ref, coef_ref, count_ref, owner_ref, other_ref, mhi_ref, mlo_ref, div_ref):
    fill(0, stencil_ref, coef_ref, count_ref, owner_ref, other_ref, mhi_ref, mlo_ref)
    cell = lax.broadcasted_iota(jnp.int32, div_ref.shape, 0)
    gain = jnp.where(cell == other_ref[...], 1.0, 0.0) - jnp.where(cell == owner_ref[...], 1.0, 0.0)
    div_ref[...] = gain.astype(BF16)


def halo_kernel(stencil_ref, coef_ref, count_ref, owner_ref, other_ref, flow_ref, ohi_ref, olo_ref,
                mhi_ref, mlo_ref, leak_ref):
    fill(1, stencil_ref, coef_ref, count_ref, owner_ref, other_ref, mhi_ref, mlo_ref)
    edges = owner_ref.shape[1]
    leaves = jnp.where(other_ref[...] < 128, 0.0, -1.0)
    levels = flow_ref.shape[0]
    parts = split(flow_ref[...] * leaves) + split(jnp.abs(flow_ref[...]) * leaves)
    leak_ref[...] = jnp.zeros_like(leak_ref)
    for part, (hi_ref, lo_ref) in enumerate(((ohi_ref, olo_ref), (mhi_ref, mlo_ref))):
        total = jnp.zeros((levels, 128), F32)
        for which in range(2):
            at = pl.ds(which * edges, edges)
            hi, lo = parts[2 * which:2 * which + 2]
            total = total + dot_nt(hi, hi_ref[:, at]) + dot_nt(lo, hi_ref[:, at]) + dot_nt(hi, lo_ref[:, at])
        leak_ref[pl.ds(0, levels), pl.ds(part * 128, 128)] = total


def product(value, mhi_ref, mlo_ref):
    hi, lo = split(value)
    both = dot(jnp.concatenate([hi, lo], axis=0), mhi_ref[...])
    return both[:value.shape[0]] + both[value.shape[0]:] + dot(hi, mlo_ref[...])


def ahead_kernel(state_ref, ohi_ref, olo_ref, picked_ref):
    picked_ref[...] = product(state_ref[...], ohi_ref, olo_ref)


def tendency(halo, picked_ref, mhi_ref, mlo_ref, div_ref, flow_ref, area_ref):
    columns = halo.shape[0]
    edges = div_ref.shape[1]
    picked = picked_ref[...] + product(halo, mhi_ref, mlo_ref)
    flow = flow_ref[...]
    flux = flow * picked[:, :edges] + jnp.abs(flow) * picked[:, edges:]
    both = dot_nt(jnp.concatenate(split(flux), axis=0), div_ref[...])
    return (both[:columns] + both[columns:]) / area_ref[...]


def halo_of(low_ref, high_ref, far_lo_ref, far_hi_ref, columns):
    return jnp.concatenate([far_lo_ref[:48], low_ref[:16], high_ref[:16], far_hi_ref[:48]], axis=0).T[:columns]


def halo_of_rows(far_lo_ref, far_hi_ref, low_ref, high_ref, columns):
    return jnp.concatenate(
        [
            low_ref[16:32], far_lo_ref[16:32], high_ref[16:32], low_ref[:16],
            high_ref[:16], low_ref[32:], far_hi_ref[16:32], high_ref[32:],
        ],
        axis=0,
    ).T[:columns]


def first_kernel(tracer_ref, lanes_ref, leak_ref, h0, h1, h2, h3, m0, m1, m2, m3, m4, m5,
                 new_ref, next_ref, prev_ref, up_ref, down_ref):
    mats = (m0, m1, m2, m3, m4, m5)
    tracer = tracer_ref[...]
    new = tracer + tendency(halo_of(h0, h1, h2, h3, tracer.shape[0]), *mats) / 3.0
    new_ref[...] = new
    put_groups(pick(new, lanes_ref[...]), next_ref, prev_ref, up_ref, down_ref)
    next_ref[48:] = leak_ref[:, 128:]
    prev_ref[48:] = leak_ref[:, 128:]


def second_kernel(levels, tracer_ref, lanes_ref, back_ref, leak_ref, h0, h1, h2, h3, m0, m1, m2, m3, m4, m5,
                  new_ref, up_ref, down_ref, next_ref, prev_ref, mass_ref):
    mats = (m0, m1, m2, m3, m4, m5)
    tracer = tracer_ref[...]
    columns = tracer.shape[0]
    new = tracer + tendency(halo_of(h0, h1, h2, h3, columns), *mats) / 2.0
    new_ref[...] = new
    put_rows(pick(new, lanes_ref[...]), up_ref, down_ref, next_ref, prev_ref)
    label = lax.broadcasted_iota(jnp.int32, (leak_ref.shape[0], 128), 1) // PEER
    shares = jnp.where(label >= 5, h2[48:], h3[48:])
    shares = jnp.where(label == 4, h0[48:], jnp.where(label == 3, h1[48:], shares))
    cell = lax.broadcasted_iota(jnp.int32, (128, 128), 0)
    owner = jnp.where(cell == back_ref[...], 1.0, 0.0).astype(BF16)
    hi, lo = split(shares)
    gain = leak_ref[:, :128] + dot_nt(hi, owner) + dot_nt(lo, owner)
    tracers = columns // levels
    row = lax.broadcasted_iota(jnp.int32, (columns, gain.shape[0]), 0) // tracers
    spread = jnp.where(row == lax.broadcasted_iota(jnp.int32, row.shape, 1), 1.0, 0.0).astype(BF16)
    hi, lo = split(gain)
    area = m5[...]
    weighted = area * tracer + (dot(spread, hi) + dot(spread, lo)) * new
    weighted = jnp.concatenate([weighted, jnp.broadcast_to(area, (128 - columns, 128))], axis=0)
    mass = jnp.sum(weighted.T, axis=0, keepdims=True)
    for device in range(mass_ref.shape[0]):
        mass_ref[device] = jnp.broadcast_to(mass, mass_ref.shape[1:])


def third_kernel(tracer_ref, rows_ref, h0, h1, h2, h3, m0, m1, m2, m3, m4, m5, out_ref, mean_ref):
    mats = (m0, m1, m2, m3, m4, m5)
    out_ref[...] = tracer_ref[...] + tendency(halo_of_rows(h0, h1, h2, h3, tracer_ref.shape[0]), *mats)
    tracers, levels = mean_ref.shape
    total = jnp.sum(rows_ref[...], axis=0)
    mean = jnp.broadcast_to(total / total[:, tracers * levels:tracers * levels + 1], (8, 128))
    lane = lax.broadcasted_iota(jnp.int32, (8, 128), 1) * tracers + lax.broadcasted_iota(jnp.int32, (8, 128), 0)
    mean_ref[...] = jnp.take_along_axis(mean, jnp.minimum(lane, 127), axis=1)[:tracers, :levels]


def relay_kernel(rows_ref, out_ref):
    total = jnp.sum(rows_ref[...], axis=0)[:1]
    for device in range(out_ref.shape[0]):
        out_ref[device] = total


def call(kernel, outs, scratch=(), **more):
    return pl.pallas_call(
        kernel,
        out_shape=outs,
        scratch_shapes=list(scratch),
        compiler_params=pltpu.CompilerParams(vmem_limit_bytes=16 * 2**20),
        **more,
    )


def array(shape, dtype=F32):
    return jax.ShapeDtypeStruct(shape, dtype)


def shift(value, by):
    count = lax.axis_size(AXES)
    return lax.ppermute(value, AXES, [(i, (i + by) % count) for i in range(count)])


def swap(value, first):
    count = lax.axis_size(AXES)
    return lax.ppermute(value, AXES, [(i, (((i - first) % count ^ 1) + first) % count) for i in range(count)])


def hop_along(after, before):
    odd = lax.axis_index("sub") % 2 == 1
    near = swap(jnp.where(odd, before, after), 0)
    far = swap(jnp.where(odd, after, before), 1)
    return jnp.where(odd, near, far), jnp.where(odd, far, near)


def hop_up(low, high, up, down, leak=None):
    width = lax.axis_size("sub")
    up = [low[16:32], up, high[16:32]]
    down = [low[32:48], down, high[32:48]]
    if leak is not None:
        label = lax.broadcasted_iota(jnp.int32, leak.shape, 1) // PEER
        up.append(jnp.where(label == 6, leak, jnp.where(label == 7, low[48:], high[48:])))
        down.append(jnp.where(label == 1, leak, jnp.where(label == 2, low[48:], high[48:])))
    return shift(jnp.concatenate(up, axis=0), width), shift(jnp.concatenate(down, axis=0), -width)


def spread_out(rows, axes, first=0):
    count = lax.axis_size(axes)
    groups = [[(first + i) % count for i in range(count)]] if first else None
    return lax.all_to_all(rows, axes, 0, 0, axis_index_groups=groups, tiled=True)


def body(tracer, edge_flow, edge_owner, edge_other, stencil, stencil_coef, stencil_count, send_cells, cell_area):
    ntracer, nlevel, cells = tracer.shape
    edges = edge_owner.shape[0]
    columns = ntracer * nlevel
    plane, depth = lax.axis_size(("core", "sub")), lax.axis_size("z")
    state = array((columns, cells))

    def messages(extra):
        return [array((48 + extra, 128)), array((48 + extra, 128)), array((PEER, 128)), array((PEER, 128))]

    whole = pl.BlockSpec(memory_space=pltpu.HBM)
    statics = [stencil, stencil_coef, stencil_count, edge_owner, edge_other, edge_flow, cell_area]
    after, before, up, down, lanes, back, rows, *statics, area = call(
        pack_kernel,
        messages(0) + [array((1, cells), jnp.int32)] * 2 + [state]
        + [array(stencil.shape, jnp.int32), array(stencil.shape), array(stencil_count.shape, jnp.int32)]
        + [array((1, edges), jnp.int32)] * 2 + [array(edge_flow.shape), array((1, cells))],
        [pltpu.VMEM(send_cells.shape, jnp.int32), pltpu.VMEM((8, cells), jnp.int32),
         pltpu.VMEM((edges,), jnp.int32), pltpu.VMEM((edges,), jnp.int32), pltpu.VMEM((cells,), F32),
         pltpu.SemaphoreType.DMA((9,))],
        in_specs=[whole] * 9,
    )(*(pltpu.with_memory_space_constraint(x, pltpu.HBM)
        for x in (tracer.transpose(1, 0, 2).reshape(columns, cells), send_cells, *statics)))
    half = [array((cells, 2 * edges), BF16)] * 2

    low, high = hop_along(after, before)
    ohi, olo, divergence = call(own_kernel, half + [array((cells, edges), BF16)])(*statics[:5])
    mhi, mlo, leak = call(halo_kernel, half + [array((32, 2 * cells))])(*statics, ohi, olo)
    low, high, mhi = lax.optimization_barrier((low, high, mhi))
    far_lo, far_hi = hop_up(low, high, up, down)
    flow = jnp.broadcast_to(statics[5][:, None, :], (nlevel, ntracer, edges)).reshape(columns, edges)
    matrices = (mhi, mlo, divergence, flow, area)
    ahead = call(ahead_kernel, array((columns, 2 * edges)))
    one, after, before, up, down = call(first_kernel, [state] + messages(32))(
        rows, lanes, leak, low, high, far_lo, far_hi, ahead(rows, ohi, olo), *matrices)

    low, high = hop_along(after, before)
    far_lo, far_hi = hop_up(low, high, up, down, leak[:, cells:])
    two, up, down, after, before, mass = call(
        functools.partial(second_kernel, nlevel), [state] + messages(0) + [array((plane, 2, 128))]
    )(rows, lanes, back, leak, low, high, far_lo, far_hi, ahead(one, ohi, olo), *matrices)

    width = lax.axis_size("sub")
    far_lo, far_hi = shift(up, width), shift(down, -width)
    mass = spread_out(mass, ("core", "sub"))
    far_lo, far_hi, mass = lax.optimization_barrier((far_lo, far_hi, mass))
    after = jnp.concatenate([after, far_lo[32:], far_hi[32:]], axis=0)
    before = jnp.concatenate([before, far_lo[:16], far_hi[:16]], axis=0)
    odd = lax.axis_index("sub") % 2 == 1
    near = swap(jnp.where(odd, before, after), 0)
    far = swap(jnp.where(odd, after, before), 1)
    mass = call(relay_kernel, array((depth, 1, 128)))(mass)
    mass = spread_out(mass, "z", 3 * depth // 4)
    near, far, mass = lax.optimization_barrier((near, far, mass))
    low, high = jnp.where(odd, near, far), jnp.where(odd, far, near)
    advected, mean = call(third_kernel, [state, array((ntracer, nlevel))])(
        rows, mass, far_lo, far_hi, low, high, ahead(two, ohi, olo), *matrices)
    return advected.reshape(nlevel, ntracer, cells).transpose(1, 0, 2), mean


def solution(mesh):
    blk, sub = mesh.devices.shape
    fine = jax.sharding.Mesh(mesh.devices.reshape(blk // 2, 2, sub), AXES)
    in_specs = (
        P(None, None, AXES), P(None, AXES), P(AXES), P(AXES), P(None, None, AXES),
        P(None, None, AXES), P(None, AXES), P(None, AXES), P(AXES),
    )
    out_specs = (P(None, None, AXES), P())
    return jax.shard_map(body, mesh=fine, in_specs=in_specs, out_specs=out_specs, check_vma=False)
```

```python
import functools

import jax
import jax.numpy as jnp
from jax import lax
from jax.experimental import pallas as pl
from jax.experimental.pallas import tpu as pltpu
from jax.sharding import PartitionSpec as P

F32 = jnp.float32
BF16 = jnp.bfloat16
PEER = 16
AXES = ("z", "core", "sub")


def split(x):
    hi = x.astype(BF16)
    return hi, (x - hi.astype(F32)).astype(BF16)


def dot(a, b):
    return lax.dot_general(a, b, (((1,), (0,)), ((), ())), preferred_element_type=F32)


def dot_nt(a, b):
    return lax.dot_general(a, b, (((1,), (1,)), ((), ())), preferred_element_type=F32)


def send_lanes(send_ref, wide_ref, backwards):
    groups, peer = send_ref.shape
    wide_ref[...] = jnp.zeros_like(wide_ref)
    wide_ref[:, :peer] = send_ref[...]
    lane = lax.broadcasted_iota(jnp.int32, (groups, 128), 1)
    group = lax.broadcasted_iota(jnp.int32, (groups, 128), 0)
    tiled = jnp.take_along_axis(wide_ref[...], lane % peer, axis=1)
    rows = []
    for back in backwards:
        want = groups - 1 - lane // peer if back else lane // peer
        rows.append(jnp.sum(jnp.where(want == group, tiled, 0), axis=0, keepdims=True))
    return rows


def square(rows):
    return jnp.concatenate([rows, jnp.zeros((128 - rows.shape[0], 128), F32)], axis=0)


def pick(state, lanes):
    return square(jnp.take_along_axis(state, jnp.broadcast_to(lanes, state.shape), axis=1)).T


def put_groups(out, next_ref, prev_ref, up_ref, down_ref):
    next_ref[:48] = jnp.concatenate([out[64:80], out[112:], out[32:48]], axis=0)
    prev_ref[:48] = jnp.concatenate([out[48:64], out[80:96], out[:16]], axis=0)
    up_ref[...] = out[96:112]
    down_ref[...] = out[16:32]


def put_rows(out, up_ref, down_ref, next_ref, prev_ref):
    up_ref[...] = out[80:]
    down_ref[...] = out[:48]
    next_ref[...] = out[64:80]
    prev_ref[...] = out[48:64]


def pack_kernel(tracer, send, stencil, coef, count, owner, other, flow, area,
                next_ref, prev_ref, up_ref, down_ref, lanes_ref, back_ref,
                tracer_ref, stencil_ref, coef_ref, count_ref, owner_ref, other_ref, flow_ref, area_ref,
                send_ref, wide_ref, owner_flat, other_flat, area_flat, sems):
    sources = (tracer, send, owner, other, area, stencil, coef, count, flow)
    targets = (tracer_ref, send_ref, owner_flat, other_flat, area_flat, stencil_ref, coef_ref, count_ref, flow_ref)
    copies = [pltpu.make_async_copy(a, b, sems.at[k]) for k, (a, b) in enumerate(zip(sources, targets))]
    for copy in copies:
        copy.start()
    copies[0].wait()
    copies[1].wait()
    lanes_ref[...], back_ref[...] = send_lanes(send_ref, wide_ref, (False, True))
    put_groups(pick(tracer_ref[...], lanes_ref[...]), next_ref, prev_ref, up_ref, down_ref)
    for copy in copies[2:]:
        copy.wait()
    owner_ref[...] = owner_flat[...].reshape(owner_ref.shape)
    other_ref[...] = other_flat[...].reshape(other_ref.shape)
    area_ref[...] = area_flat[...].reshape(area_ref.shape)


def fill(part, stencil_ref, coef_ref, count_ref, owner_ref, other_ref, mhi_ref, mlo_ref):
    edges = owner_ref.shape[1]
    for chunk in range(edges // 128):
        at = pl.ds(chunk * 128, 128)
        cell = lax.broadcasted_iota(jnp.int32, (128, 128), 0) + part * 128
        curves = []
        for side in range(2):
            total = jnp.zeros((128, 128), F32)
            count = count_ref[pl.ds(side, 1), at]
            for j in range(stencil_ref.shape[1]):
                weight = jnp.where(j < count, coef_ref[side, pl.ds(j, 1), at], 0.0)
                index = stencil_ref[side, pl.ds(j, 1), at]
                total = total + jnp.where(cell == index, weight, 0.0)
            curves.append(total)
        ends = jnp.where(cell == other_ref[:, at], 0.5, 0.0)
        if part == 0:
            ends = ends + jnp.where(cell == owner_ref[:, at], 0.5, 0.0)
        mean = ends - (curves[0] + curves[1]) * (1.0 / 12.0)
        diff = (curves[0] - curves[1]) * (1.0 / 12.0)
        for which, value in enumerate((mean, diff)):
            columns = pl.ds(which * edges + chunk * 128, 128)
            mhi_ref[:, columns], mlo_ref[:, columns] = split(value)


def own_kernel(stencil_ref, coef_ref, count_ref, owner_ref, other_ref, mhi_ref, mlo_ref, div_ref):
    fill(0, stencil_ref, coef_ref, count_ref, owner_ref, other_ref, mhi_ref, mlo_ref)
    cell = lax.broadcasted_iota(jnp.int32, div_ref.shape, 0)
    gain = jnp.where(cell == other_ref[...], 1.0, 0.0) - jnp.where(cell == owner_ref[...], 1.0, 0.0)
    div_ref[...] = gain.astype(BF16)


def halo_kernel(stencil_ref, coef_ref, count_ref, owner_ref, other_ref, flow_ref, ohi_ref, olo_ref,
                mhi_ref, mlo_ref, leak_ref):
    fill(1, stencil_ref, coef_ref, count_ref, owner_ref, other_ref, mhi_ref, mlo_ref)
    edges = owner_ref.shape[1]
    leaves = jnp.where(other_ref[...] < 128, 0.0, -1.0)
    levels = flow_ref.shape[0]
    parts = split(flow_ref[...] * leaves) + split(jnp.abs(flow_ref[...]) * leaves)
    leak_ref[...] = jnp.zeros_like(leak_ref)
    for part, (hi_ref, lo_ref) in enumerate(((ohi_ref, olo_ref), (mhi_ref, mlo_ref))):
        total = jnp.zeros((levels, 128), F32)
        for which in range(2):
            at = pl.ds(which * edges, edges)
            hi, lo = parts[2 * which:2 * which + 2]
            total = total + dot_nt(hi, hi_ref[:, at]) + dot_nt(lo, hi_ref[:, at]) + dot_nt(hi, lo_ref[:, at])
        leak_ref[pl.ds(0, levels), pl.ds(part * 128, 128)] = total


def product(value, mhi_ref, mlo_ref):
    hi, lo = split(value)
    both = dot(jnp.concatenate([hi, lo], axis=0), mhi_ref[...])
    return both[:value.shape[0]] + both[value.shape[0]:] + dot(hi, mlo_ref[...])


def ahead_kernel(state_ref, ohi_ref, olo_ref, picked_ref):
    picked_ref[...] = product(state_ref[...], ohi_ref, olo_ref)


def tendency(halo, picked_ref, mhi_ref, mlo_ref, div_ref, flow_ref, area_ref):
    columns = halo.shape[0]
    edges = div_ref.shape[1]
    picked = picked_ref[...] + product(halo, mhi_ref, mlo_ref)
    flow = flow_ref[...]
    flux = flow * picked[:, :edges] + jnp.abs(flow) * picked[:, edges:]
    both = dot_nt(jnp.concatenate(split(flux), axis=0), div_ref[...])
    return (both[:columns] + both[columns:]) / area_ref[...]


def halo_of(low_ref, high_ref, far_lo_ref, far_hi_ref, columns):
    return jnp.concatenate([far_lo_ref[:48], low_ref[:16], high_ref[:16], far_hi_ref[:48]], axis=0).T[:columns]


def halo_of_rows(far_lo_ref, far_hi_ref, low_ref, high_ref, columns):
    return jnp.concatenate(
        [
            low_ref[16:32], far_lo_ref[16:32], high_ref[16:32], low_ref[:16],
            high_ref[:16], low_ref[32:], far_hi_ref[16:32], high_ref[32:],
        ],
        axis=0,
    ).T[:columns]


def first_kernel(tracer_ref, lanes_ref, leak_ref, h0, h1, h2, h3, m0, m1, m2, m3, m4, m5,
                 new_ref, next_ref, prev_ref, up_ref, down_ref):
    mats = (m0, m1, m2, m3, m4, m5)
    tracer = tracer_ref[...]
    new = tracer + tendency(halo_of(h0, h1, h2, h3, tracer.shape[0]), *mats) / 3.0
    new_ref[...] = new
    put_groups(pick(new, lanes_ref[...]), next_ref, prev_ref, up_ref, down_ref)
    next_ref[48:] = leak_ref[:, 128:]
    prev_ref[48:] = leak_ref[:, 128:]


def second_kernel(levels, tracer_ref, lanes_ref, back_ref, leak_ref, h0, h1, h2, h3, m0, m1, m2, m3, m4, m5,
                  new_ref, up_ref, down_ref, next_ref, prev_ref, mass_ref, mass_rows, sem):
    mats = (m0, m1, m2, m3, m4, m5)
    tracer = tracer_ref[...]
    columns = tracer.shape[0]
    new = tracer + tendency(halo_of(h0, h1, h2, h3, columns), *mats) / 2.0
    new_ref[...] = new
    label = lax.broadcasted_iota(jnp.int32, (leak_ref.shape[0], 128), 1) // PEER
    shares = jnp.where(label >= 5, h2[48:], h3[48:])
    shares = jnp.where(label == 4, h0[48:], jnp.where(label == 3, h1[48:], shares))
    cell = lax.broadcasted_iota(jnp.int32, (128, 128), 0)
    owner = jnp.where(cell == back_ref[...], 1.0, 0.0).astype(BF16)
    hi, lo = split(shares)
    gain = leak_ref[:, :128] + dot_nt(hi, owner) + dot_nt(lo, owner)
    tracers = columns // levels
    row = lax.broadcasted_iota(jnp.int32, (columns, gain.shape[0]), 0) // tracers
    spread = jnp.where(row == lax.broadcasted_iota(jnp.int32, row.shape, 1), 1.0, 0.0).astype(BF16)
    hi, lo = split(gain)
    area = m5[...]
    weighted = area * tracer + (dot(spread, hi) + dot(spread, lo)) * new
    weighted = jnp.concatenate([weighted, jnp.broadcast_to(area, (128 - columns, 128))], axis=0)
    mass = jnp.sum(weighted.T, axis=0, keepdims=True)
    for device in range(mass_rows.shape[0]):
        mass_rows[device] = jnp.broadcast_to(mass, mass_rows.shape[1:])
    copy = pltpu.make_async_copy(mass_rows, mass_ref, sem)
    copy.start()
    put_rows(pick(new, lanes_ref[...]), up_ref, down_ref, next_ref, prev_ref)
    copy.wait()


def third_kernel(tracer_ref, rows_ref, h0, h1, h2, h3, m0, m1, m2, m3, m4, m5, out_ref, mean_ref, rows_out, sem):
    mats = (m0, m1, m2, m3, m4, m5)
    rows_out[...] = tracer_ref[...] + tendency(halo_of_rows(h0, h1, h2, h3, tracer_ref.shape[0]), *mats)
    copy = pltpu.make_async_copy(rows_out, out_ref, sem)
    copy.start()
    tracers, levels = mean_ref.shape
    total = jnp.sum(rows_ref[...], axis=0)
    mean = jnp.broadcast_to(total / total[:, tracers * levels:tracers * levels + 1], (8, 128))
    lane = lax.broadcasted_iota(jnp.int32, (8, 128), 1) * tracers + lax.broadcasted_iota(jnp.int32, (8, 128), 0)
    mean_ref[...] = jnp.take_along_axis(mean, jnp.minimum(lane, 127), axis=1)[:tracers, :levels]
    copy.wait()


def relay_kernel(rows_ref, out_ref):
    total = jnp.sum(rows_ref[...], axis=0)[:1]
    for device in range(out_ref.shape[0]):
        out_ref[device] = total


def call(kernel, outs, scratch=(), **more):
    return pl.pallas_call(
        kernel,
        out_shape=outs,
        scratch_shapes=list(scratch),
        compiler_params=pltpu.CompilerParams(vmem_limit_bytes=16 * 2**20),
        **more,
    )


def array(shape, dtype=F32):
    return jax.ShapeDtypeStruct(shape, dtype)


def shift(value, by):
    count = lax.axis_size(AXES)
    return lax.ppermute(value, AXES, [(i, (i + by) % count) for i in range(count)])


def swap(value, first):
    count = lax.axis_size(AXES)
    return lax.ppermute(value, AXES, [(i, (((i - first) % count ^ 1) + first) % count) for i in range(count)])


def hop_along(after, before):
    odd = lax.axis_index("sub") % 2 == 1
    near = swap(jnp.where(odd, before, after), 0)
    far = swap(jnp.where(odd, after, before), 1)
    return jnp.where(odd, near, far), jnp.where(odd, far, near)


def hop_up(low, high, up, down, leak=None):
    width = lax.axis_size("sub")
    up = [low[16:32], up, high[16:32]]
    down = [low[32:48], down, high[32:48]]
    if leak is not None:
        label = lax.broadcasted_iota(jnp.int32, leak.shape, 1) // PEER
        up.append(jnp.where(label == 6, leak, jnp.where(label == 7, low[48:], high[48:])))
        down.append(jnp.where(label == 1, leak, jnp.where(label == 2, low[48:], high[48:])))
    return shift(jnp.concatenate(up, axis=0), width), shift(jnp.concatenate(down, axis=0), -width)


def spread_out(rows, axes, first=0):
    count = lax.axis_size(axes)
    groups = [[(first + i) % count for i in range(count)]] if first else None
    return lax.all_to_all(rows, axes, 0, 0, axis_index_groups=groups, tiled=True)


def body(tracer, edge_flow, edge_owner, edge_other, stencil, stencil_coef, stencil_count, send_cells, cell_area):
    ntracer, nlevel, cells = tracer.shape
    edges = edge_owner.shape[0]
    columns = ntracer * nlevel
    plane, depth = lax.axis_size(("core", "sub")), lax.axis_size("z")
    state = array((columns, cells))

    def messages(extra):
        return [array((48 + extra, 128)), array((48 + extra, 128)), array((PEER, 128)), array((PEER, 128))]

    whole = pl.BlockSpec(memory_space=pltpu.HBM)
    statics = [stencil, stencil_coef, stencil_count, edge_owner, edge_other, edge_flow, cell_area]
    after, before, up, down, lanes, back, rows, *statics, area = call(
        pack_kernel,
        messages(0) + [array((1, cells), jnp.int32)] * 2 + [state]
        + [array(stencil.shape, jnp.int32), array(stencil.shape), array(stencil_count.shape, jnp.int32)]
        + [array((1, edges), jnp.int32)] * 2 + [array(edge_flow.shape), array((1, cells))],
        [pltpu.VMEM(send_cells.shape, jnp.int32), pltpu.VMEM((8, cells), jnp.int32),
         pltpu.VMEM((edges,), jnp.int32), pltpu.VMEM((edges,), jnp.int32), pltpu.VMEM((cells,), F32),
         pltpu.SemaphoreType.DMA((9,))],
        in_specs=[whole] * 9,
    )(*(pltpu.with_memory_space_constraint(x, pltpu.HBM)
        for x in (tracer.transpose(1, 0, 2).reshape(columns, cells), send_cells, *statics)))
    half = [array((cells, 2 * edges), BF16)] * 2

    low, high = hop_along(after, before)
    ohi, olo, divergence = call(own_kernel, half + [array((cells, edges), BF16)])(*statics[:5])
    mhi, mlo, leak = call(halo_kernel, half + [array((32, 2 * cells))])(*statics, ohi, olo)
    low, high, mhi = lax.optimization_barrier((low, high, mhi))
    far_lo, far_hi = hop_up(low, high, up, down)
    flow = jnp.broadcast_to(statics[5][:, None, :], (nlevel, ntracer, edges)).reshape(columns, edges)
    matrices = (mhi, mlo, divergence, flow, area)
    ahead = call(ahead_kernel, array((columns, 2 * edges)))
    one, after, before, up, down = call(first_kernel, [state] + messages(32))(
        rows, lanes, leak, low, high, far_lo, far_hi, ahead(rows, ohi, olo), *matrices)

    low, high = hop_along(after, before)
    far_lo, far_hi = hop_up(low, high, up, down, leak[:, cells:])
    two, up, down, after, before, mass = call(
        functools.partial(second_kernel, nlevel), [state] + messages(0) + [array((plane, 2, 128))],
        [pltpu.VMEM((plane, 2, 128), F32), pltpu.SemaphoreType.DMA],
        out_specs=[pl.BlockSpec(memory_space=pltpu.VMEM)] * 5 + [pl.BlockSpec(memory_space=pltpu.HBM)],
    )(rows, lanes, back, leak, low, high, far_lo, far_hi, ahead(one, ohi, olo), *matrices)

    width = lax.axis_size("sub")
    far_lo, far_hi = shift(up, width), shift(down, -width)
    mass = spread_out(mass, ("core", "sub"))
    far_lo, far_hi, mass = lax.optimization_barrier((far_lo, far_hi, mass))
    after = jnp.concatenate([after, far_lo[32:], far_hi[32:]], axis=0)
    before = jnp.concatenate([before, far_lo[:16], far_hi[:16]], axis=0)
    odd = lax.axis_index("sub") % 2 == 1
    near = swap(jnp.where(odd, before, after), 0)
    far = swap(jnp.where(odd, after, before), 1)
    mass = call(relay_kernel, array((depth, 1, 128)))(mass)
    mass = spread_out(mass, "z", 3 * depth // 4)
    near, far, mass = lax.optimization_barrier((near, far, mass))
    low, high = jnp.where(odd, near, far), jnp.where(odd, far, near)
    advected, mean = call(
        third_kernel, [state, array((ntracer, nlevel))], [pltpu.VMEM((columns, cells), F32), pltpu.SemaphoreType.DMA],
        out_specs=[pl.BlockSpec(memory_space=pltpu.HBM), pl.BlockSpec(memory_space=pltpu.VMEM)],
    )(
        rows, mass, far_lo, far_hi, low, high, ahead(two, ohi, olo), *matrices)
    return advected.reshape(nlevel, ntracer, cells).transpose(1, 0, 2), mean


def solution(mesh):
    blk, sub = mesh.devices.shape
    fine = jax.sharding.Mesh(mesh.devices.reshape(blk // 2, 2, sub), AXES)
    in_specs = (
        P(None, None, AXES), P(None, AXES), P(AXES), P(AXES), P(None, None, AXES),
        P(None, None, AXES), P(None, AXES), P(None, AXES), P(AXES),
    )
    out_specs = (P(None, None, AXES), P())
    return jax.shard_map(body, mesh=fine, in_specs=in_specs, out_specs=out_specs, check_vma=False)
```
